256 devices in a mesh: tm: 32 (over x, y, core), space: 8 (over z).
Axes of the slice: x: 4, y: 4, z: 8, core: 2. Of those that a mesh axis runs over, the one named last changes fastest.
Arguments:
- starts: float32 [32, 3, 32, 128, 128], P('tm', None, 'space'), may hold values from 0 to 2
- velocity: float32 [3, 32, 128, 128], P(None, 'space'), may hold values from -1 to 1
- diffusivity: float32 [32, 128, 128], P('space'), may hold values from 0.2 to 0.8
- rate: float32 [32, 128, 128], P('space'), may hold values from 0.2 to 1
Outputs:
- new_starts: float32 [32, 3, 32, 128, 128], P('tm', None, 'space')
- new_ends: float32 [32, 3, 32, 128, 128], P('tm', None, 'space')
The draws below stay inside these ranges and needn't reach their ends.
All inputs are finite; a program needn't handle non-finite values.
Results may differ from the reference program's by a relative error of at most 0.000029.
Values sent between devices are 32-bit elements; how exact they have to be, the bound alone decides.
No kernel may reach another device: no remote copies, remote signals or barrier semaphores. Data moves between devices by JAX's collectives and lax.ppermute only.
A program may use at most 128 MiB of HBM per device.

```python
import jax
import jax.numpy as jnp
from jax import lax

NX = 128
NY = 128
FINE = 8
COARSE_STEPS = 2
SPECIES = 3
NZ = 32
SLICES = 32


def steps_of(stream_key, shape, split, low, top_value):
    gain, own = 1.0, jax.random.fold_in(stream_key, 6)
    for axis_at, shards_of in split:
        draws = jnp.exp(jax.random.uniform(jax.random.fold_in(own, axis_at), (shards_of,), jnp.float32, low / len(split), top_value / len(split)))
        gain = gain * jnp.repeat(draws, shape[axis_at] // shards_of).reshape([-1 if axis == axis_at else 1 for axis in range(len(shape))])
    return gain


def setup_inputs(seed: int = 0) -> dict:
    key_list = jax.random.split(jax.random.key(seed), 5)
    return {
        "starts": jnp.clip(2.0 * jax.random.uniform(key_list[0], (SLICES, SPECIES, NZ, NY, NX), jnp.float32) ** steps_of(key_list[0], (SLICES, SPECIES, NZ, NY, NX), ((0, 32), (2, 8)), -0.2, 0.2), 0.0, 2.0),
        "velocity": jnp.clip(jax.random.uniform(key_list[1], (3, NZ, NY, NX), jnp.float32, -1.0, 1.0) * steps_of(key_list[1], (3, NZ, NY, NX), ((1, 8),), -0.4, 0.0), -1.0, 1.0),
        "diffusivity": jnp.clip(0.2 + 0.6 * jax.random.uniform(key_list[2], (NZ, NY, NX), jnp.float32) ** steps_of(key_list[2], (NZ, NY, NX), ((0, 8),), -0.2, 0.2), 0.2, 0.8),
        "rate": jnp.clip(0.2 + 0.8 * jax.random.uniform(key_list[3], (NZ, NY, NX), jnp.float32) ** steps_of(key_list[3], (NZ, NY, NX), ((0, 8),), -0.2, 0.2), 0.2, 1.0),
    }


species_weights = (1.0, 0.6, 0.3)
decay_rate = 0.5


def stencil(padded, coefs, inv_h, step_dt):
    center = padded[:, 1:-1]
    lower = padded[:, :-2]
    upper = padded[:, 2:]
    x_minus = jnp.roll(center, 1, axis=3)
    x_plus = jnp.roll(center, -1, axis=3)
    y_minus = jnp.roll(center, 1, axis=2)
    y_plus = jnp.roll(center, -1, axis=2)
    laplace = (x_minus + x_plus + y_minus + y_plus + lower + upper - 6.0 * center) * (inv_h * inv_h)
    vel_x = coefs[0][None]
    vel_y = coefs[1][None]
    vel_z = coefs[2][None]
    advect = (jnp.maximum(vel_x, 0.0) * (center - x_minus) + jnp.minimum(vel_x, 0.0) * (x_plus - center)
              + jnp.maximum(vel_y, 0.0) * (center - y_minus) + jnp.minimum(vel_y, 0.0) * (y_plus - center)
              + jnp.maximum(vel_z, 0.0) * (center - lower) + jnp.minimum(vel_z, 0.0) * (upper - center)) * inv_h
    weights = jnp.array(species_weights, jnp.float32)[:, None, None, None]
    diffuse = weights * coefs[3][None] * laplace
    react_term = coefs[4] * center[0] * center[1]
    react = jnp.stack([-react_term, -react_term, react_term - decay_rate * center[2]], 0)
    return center + step_dt * (diffuse - advect + react)


def restrict(values):
    comps, depth, rows, cols = values.shape
    blocks = values.reshape(comps, depth // 4, 4, rows // 4, 4, cols // 4, 4)
    return jnp.mean(blocks, axis=(2, 4, 6))


def prolong(coarse_vals):
    comps, depth, rows, cols = coarse_vals.shape
    wide = jnp.broadcast_to(coarse_vals[:, :, None, :, None, :, None], (comps, depth, 4, rows, 4, cols, 4))
    return wide.reshape(comps, depth * 4, rows * 4, cols * 4)


def zero_pad(state):
    return jnp.pad(state, ((0, 0), (1, 1), (0, 0), (0, 0)))


def coarse_prop(state, coarse_coefs):
    for _ in range(COARSE_STEPS):
        state = stencil(zero_pad(state), coarse_coefs, 0.25, 0.4)
    return state


def reference(starts, velocity, diffusivity, rate):
    coefs = jnp.concatenate([velocity, diffusivity[None], rate[None]], 0)
    coarse_coefs = restrict(coefs)

    def fine_prop(state):
        for _ in range(FINE):
            state = stencil(zero_pad(state), coefs, 1.0, 0.1)
        return state

    ends = lax.map(fine_prop, starts)
    start_coarse = lax.map(restrict, starts)
    end_coarse = lax.map(restrict, ends)
    old_coarse = lax.map(lambda state: coarse_prop(state, coarse_coefs), start_coarse)
    defect = end_coarse - old_coarse

    def link(state, pair):
        old_val, defect_val = pair
        advanced = coarse_prop(state, coarse_coefs)
        return advanced + defect_val, advanced - old_val

    _, correction = lax.scan(link, start_coarse[0], (old_coarse, defect))
    new_ends = ends + lax.map(prolong, correction)
    new_starts = jnp.concatenate([starts[:1], new_ends[:-1]], 0)
    return (new_starts, new_ends)
```

```python
import functools

import jax
import jax.numpy as jnp
import numpy as np
from jax import lax
from jax.experimental import pallas as pl
from jax.experimental.pallas import tpu as pltpu
from jax.sharding import PartitionSpec as P


SPECIES_K = (1.0, 0.6, 0.3)
DECAY = 0.5
FINE_DT = 0.1
COARSE_Q = 0.25
COARSE_DT = 0.4
HALF = 4
VMEM_BYTES = 48 * 1024 * 1024
F32 = jnp.float32
EXACT = lax.Precision.HIGHEST


def coarse_maps(comps):
    x = np.arange(128)
    lane = np.arange(128)
    spread = (x[:, None] // 4 == lane[None, :] // 4).astype(np.float32)
    comp, yv, s = np.meshgrid(np.arange(comps), np.arange(4), np.arange(8), indexing="ij")
    row_to = (comp * 8 + 4 * (s % 2) + yv).reshape(-1)
    fold = (np.arange(comps * 8)[:, None] == row_to[None, :]).astype(np.float32)
    keep = ((s // 2).reshape(-1)[:, None] == lane[None, :] % 4).astype(np.float32)
    return spread, fold, keep


def fold_rows(rows, spread, fold, keep):
    wide = jnp.dot(rows, spread, precision=EXACT, preferred_element_type=F32) * keep
    return jnp.dot(fold, wide, precision=EXACT, preferred_element_type=F32) * (1.0 / 64.0)


def unfold_rows(coarse, spread, fold, keep):
    wide = lax.dot_general(
        fold, coarse, (((0,), (0,)), ((), ())), precision=EXACT, preferred_element_type=F32
    )
    return lax.dot_general(
        wide * keep, spread, (((1,), (1,)), ((), ())), precision=EXACT, preferred_element_type=F32
    )


def block_rows(load, comps):
    out = []
    for comp in range(comps):
        for yv in range(4):
            parts = [load(comp, z, 4 * yv + j) for z in range(4) for j in range(4)]
            while len(parts) > 1:
                parts = [a + b for a, b in zip(parts[::2], parts[1::2])]
            out.append(parts[0])
    return jnp.concatenate(out, 0)


def strided(ref, *lead):
    return lambda v: ref[(*lead, pl.ds(v, 8, stride=16), slice(None))]


def prep_kernel(starts, vel, dif, rate, spread, fold, keep, out):
    def load(comp, z, v):
        if comp < 3:
            return strided(starts, comp, z)(v)
        if comp < 6:
            return strided(vel, comp - 3, z)(v)
        return strided(dif if comp == 6 else rate, z)(v)

    own = fold_rows(block_rows(load, 8), spread[...], fold[...], keep[...])
    for z in range(8):
        out[z] = own


def fine_kernel(native, *refs):
    if native:
        (pos, own, low, high, vel, dif, rate, c_low, c_high, out, cf, buf_a, buf_b) = refs
    else:
        (pos, own, low, high, vel, dif, rate, c_low, c_high, old, spread, fold, keep,
         out, mine, sent, cf, buf_a, buf_b) = refs
    z_at = pos[1]
    has_low = jnp.where(z_at > 0, 1.0, 0.0).astype(F32)
    has_high = jnp.where(z_at < pos[2] - 1, 1.0, 0.0).astype(F32)

    def prepare(plane, loads, scale):
        for v in range(16):
            vx, vy, vz, d, r = [f(v) for f in loads]
            total = None
            for i, w in enumerate((vx, vy, vz)):
                w = w * (FINE_DT * scale)
                up = jnp.maximum(w, 0.0)
                down = up - w
                cf[plane, 2 * i, v] = up
                cf[plane, 2 * i + 1, v] = down
                both = up + down
                total = both if total is None else total + both
            cf[plane, 6, v] = d * (FINE_DT * scale)
            cf[plane, 7, v] = r * (FINE_DT * scale)
            cf[plane, 8, v] = 1.0 - total

    @pl.loop(0, 3)
    def _(z):
        prepare(z, [strided(c_low, c, z) for c in range(5)], has_low)
        prepare(z + 7, [strided(c_high, c, z) for c in range(5)], has_high)

    @pl.loop(0, 4)
    def _(z):
        prepare(z + 3, [strided(vel, c, z) for c in range(3)] + [strided(dif, z), strided(rate, z)], 1.0)

    @pl.loop(0, 4)
    def _(z):
        for src, at, scale in ((low, 0, has_low), (own, 4, None), (high, 8, has_high)):
            for sp in range(3):
                for v in range(16):
                    val = strided(src, sp, z)(v) if native else src[sp, z, v]
                    buf_a[sp, z + at, v] = val if scale is None else val * scale

    def step(src, dst, lo, hi):
        @pl.loop(lo, hi)
        def _(p):
            rows = [[src[sp, p, v] for v in range(16)] for sp in range(3)]
            for v in range(16):
                w = [cf[p - 1, i, v] for i in range(9)]
                d = w[6]
                new = []
                for sp in range(3):
                    u = rows[sp][v]
                    below = rows[sp][v - 1] if v > 0 else pltpu.roll(rows[sp][15], 1, 0)
                    above = rows[sp][v + 1] if v < 15 else pltpu.roll(rows[sp][0], 7, 0)
                    near = (
                        pltpu.roll(u, 1, 1), pltpu.roll(u, 127, 1),
                        below, above,
                        src[sp, p - 1, v], src[sp, p + 1, v],
                    )
                    flow = (w[0] * near[0] + w[1] * near[1]) + (w[2] * near[2] + w[3] * near[3]) + (
                        w[4] * near[4] + w[5] * near[5])
                    lap = (near[0] + near[1]) + (near[2] + near[3]) + (near[4] + near[5])
                    k = SPECIES_K[sp]
                    mid = w[8] - d * (6.0 * k)
                    if sp == 2:
                        mid = mid - FINE_DT * DECAY
                    new.append(mid * u + (d * k if k != 1.0 else d) * lap + flow)
                r = w[7] * rows[0][v] * rows[1][v]
                for sp, val in enumerate((new[0] - r, new[1] - r, new[2] + r)):
                    dst[sp, p, v] = val

    step(buf_a, buf_b, 1, 11)
    step(buf_b, buf_a, 2, 10)
    step(buf_a, buf_b, 3, 9)
    step(buf_b, buf_a, 4, 8)

    if native:
        for sp in range(3):
            out[sp] = buf_a[sp, 4:8]
        return
    part = fold_rows(
        block_rows(lambda sp, z, v: buf_a[sp, 4 + z, v], 3), spread[...], fold[...], keep[...]
    )
    back = unfold_rows(part, spread[...], fold[...], keep[...])
    for sp in range(3):
        for yv in range(4):
            at = (sp * 4 + yv) * 8
            cell = back[at:at + 8]
            for z in range(4):
                for j in range(4):
                    v = 4 * yv + j
                    out[sp, z, v] = buf_a[sp, 4 + z, v] - cell
    mine[...] = part
    here = lax.broadcasted_iota(jnp.int32, (24, 8, 128), 1) == z_at
    before = jnp.sum(jnp.where(here, old[...], 0.0), axis=1)
    diff = part - before
    for z in range(8):
        sent[z] = diff


def coarse_step(load, cf, store):
    lane = lax.broadcasted_iota(jnp.int32, (8, 128), 1) % 4
    rows = [[load(sp, y) for y in range(8)] for sp in range(3)]
    for y in range(8):
        new = []
        for sp in range(3):
            u = rows[sp][y]
            if y > 0:
                below = rows[sp][y - 1]
            else:
                below = jnp.where(lane == 0, pltpu.roll(rows[sp][7], 125, 1), pltpu.roll(rows[sp][7], 1, 1))
            if y < 7:
                above = rows[sp][y + 1]
            else:
                above = jnp.where(lane == 3, pltpu.roll(rows[sp][0], 3, 1), pltpu.roll(rows[sp][0], 127, 1))
            w = [cf[7 * sp + i, y] for i in range(7)]
            val = (w[6] * u + w[2] * below) + (w[3] * above + w[0] * pltpu.roll(u, 4, 1)) + (
                w[1] * pltpu.roll(u, 124, 1) + (w[4] * pltpu.roll(u, 1, 0) + w[5] * pltpu.roll(u, 7, 0)))
            new.append(val)
        r = cf[21, y] * rows[0][y] * rows[1][y]
        store(0, y, new[0] - r)
        store(1, y, new[1] - r)
        store(2, y, new[2] + r)


def old_kernel(pos, got, cf, old, tmp):
    slice_at = pos[0]
    sub = lax.broadcasted_iota(jnp.int32, (8, 128), 0)

    def row(r):
        return got[pl.ds(r, 8, stride=64), :]

    for y in range(8):
        vel = [row(24 + 8 * c + y) * (COARSE_DT * COARSE_Q) for c in range(3)]
        d = row(48 + y) * (COARSE_DT * COARSE_Q * COARSE_Q)
        up = [jnp.maximum(v, 0.0) for v in vel]
        down = [a - v for a, v in zip(up, vel)]
        for sp, k in enumerate(SPECIES_K):
            kd = d * k
            total = 6.0 * kd
            for c in range(3):
                total = total + up[c] + down[c]
                lo, hi = kd + up[c], kd + down[c]
                if c == 2:
                    lo = jnp.where(sub == 0, 0.0, lo)
                    hi = jnp.where(sub == 7, 0.0, hi)
                cf[7 * sp + 2 * c, y] = lo
                cf[7 * sp + 2 * c + 1, y] = hi
            mid = 1.0 - total
            if sp == 2:
                mid = mid - COARSE_DT * DECAY
            cf[7 * sp + 6, y] = mid
        cf[21, y] = row(56 + y) * COARSE_DT

    def put(sp, y, val):
        tmp[8 * sp + y] = val

    def put_old(sp, y, val):
        old[8 * sp + y] = jnp.where(slice_at == 0, 0.0, val)

    coarse_step(lambda sp, y: row(8 * sp + y), cf, put)
    coarse_step(lambda sp, y: tmp[8 * sp + y], cf, put_old)


def chain_kernel(turn, pos, c_in, kept, cf, *refs):
    defects, (c_out, keep, state, tmp, line) = refs[:8], refs[8:]
    group, at_y, core = pos[3], pos[4], pos[5]

    @pl.when(group != turn)
    def _():
        c_out[...] = c_in[...]
        keep[...] = kept[...]

    @pl.when(group == turn)
    def _():
        for k in range(4):
            slot = lax.rem(at_y - k + 4, 4) * 2
            line[slot + core] = defects[k][...]
            line[slot + 1 - core] = defects[4 + k][...]
        state[...] = jnp.zeros_like(state) if turn == 0 else c_in[...]
        own = 2 * at_y + core

        def put(ref):
            def store(sp, y, val):
                ref[8 * sp + y] = val
            return store

        @pl.loop(0, 8)
        def _(i):
            @pl.when(i == own)
            def _():
                keep[0] = state[...]

            def add(sp, y, val):
                r = 8 * sp + y
                state[r] = val + line[i, pl.ds(r, 8, stride=24), :]

            coarse_step(lambda sp, y: state[8 * sp + y], cf, put(tmp))
            coarse_step(lambda sp, y: tmp[8 * sp + y], cf, add)

            @pl.when(i == own)
            def _():
                keep[1] = state[...]

        c_out[...] = state[...]


def last_kernel(pos, ends, arrived, keep_c, starts, spread, fold, keep, new_starts, new_ends):
    z_at, slice_at = pos[1], pos[0]
    here = lax.broadcasted_iota(jnp.int32, (24, 8, 128), 1) == z_at
    for which, src, dst in ((1, ends, new_ends), (0, arrived, new_starts)):
        own = jnp.sum(jnp.where(here, keep_c[which], 0.0), axis=1)
        back = unfold_rows(own, spread[...], fold[...], keep[...])
        for sp in range(3):
            for yv in range(4):
                at = (sp * 4 + yv) * 8
                cell = back[at:at + 8]
                for z in range(4):
                    for j in range(4):
                        v = 4 * yv + j
                        dst[sp, z, pl.ds(v, 8, stride=16), :] = src[sp, z, v] + cell

    @pl.when(slice_at == 0)
    def _():
        new_starts[...] = starts[...]


def call(kernel, outs, scratch, *args, smem=True):
    specs = [pl.BlockSpec(memory_space=pltpu.VMEM)] * len(args)
    if smem:
        specs[0] = pl.BlockSpec(memory_space=pltpu.SMEM)
    return pl.pallas_call(
        kernel,
        out_shape=[jax.ShapeDtypeStruct(s, F32) for s in outs],
        in_specs=specs,
        out_specs=[pl.BlockSpec(memory_space=pltpu.VMEM)] * len(outs),
        scratch_shapes=[pltpu.VMEM(s, F32) for s in scratch],
        compiler_params=pltpu.CompilerParams(vmem_limit_bytes=VMEM_BYTES),
    )(*args)


def over_z(block, shift):
    count = lax.axis_size("space")
    return lax.ppermute(block, "space", [(i, (i + shift) % count) for i in range(count)])


def over_tm(block, move):
    pairs = []
    for i in range(32):
        x, y, c = i // 8, i // 2 % 4, i % 2
        x, y, c = move(x, y, c)
        pairs.append((i, (x % 4) * 8 + (y % 4) * 2 + c))
    return lax.ppermute(block, "tm", pairs)


def shards(starts, velocity, diffusivity, rate):
    slab = starts[0]
    slice_at = lax.axis_index("tm")
    z_at = lax.axis_index("space")
    pos = jnp.stack(
        [slice_at, z_at, lax.axis_size("space"), slice_at // 8, slice_at // 2 % 4, slice_at % 2]
    ).astype(jnp.int32)
    coefs = jnp.concatenate([velocity, diffusivity[None], rate[None]], 0)

    c_low = over_z(coefs[:, 1:], 1)
    c_high = over_z(coefs[:, :3], -1)
    low = over_z(slab, 1)
    high = over_z(slab, -1)

    maps8 = [jnp.asarray(m) for m in coarse_maps(8)]
    maps3 = [jnp.asarray(m) for m in coarse_maps(3)]
    (thin,) = call(prep_kernel, [(8, 64, 128)], [], slab, velocity, diffusivity, rate, *maps8, smem=False)
    full = lax.all_to_all(thin, "space", 0, 0, tiled=True)
    coarse_cf, old = call(
        old_kernel, [(22, 8, 8, 128), (24, 8, 128)], [(24, 8, 128)], pos, full.reshape(512, 128)
    )

    fine_scratch = [(10, 9, 16, 8, 128), (3, 12, 16, 8, 128), (3, 12, 16, 8, 128)]
    (middle,) = call(
        functools.partial(fine_kernel, True), [(3, 4, 16, 8, 128)], fine_scratch,
        pos, slab, low, high, velocity, diffusivity, rate, c_low, c_high,
    )
    low = over_z(middle, 1)
    high = over_z(middle, -1)
    ends, _, diff = call(
        functools.partial(fine_kernel, False),
        [(3, 4, 16, 8, 128), (24, 128), (8, 24, 128)], fine_scratch,
        pos, middle, low, high, velocity, diffusivity, rate, c_low, c_high, old, *maps3,
    )

    arrived = over_tm(ends, lambda x, y, c: (x + (y + c) // 4, y + c, 1 - c))
    defect = lax.all_to_all(diff, "space", 0, 0, tiled=True).reshape(192, 128)
    rows = [defect] + [over_tm(defect, lambda x, y, c, k=k: (x, y + k, c)) for k in (1, 2, 3)]
    rows += [over_tm(r, lambda x, y, c: (x, y, 1 - c)) for r in rows]

    state = jnp.zeros((24, 8, 128), F32)
    kept = jnp.zeros((2, 24, 8, 128), F32)
    for turn in range(4):
        state, kept = call(
            functools.partial(chain_kernel, turn),
            [(24, 8, 128), (2, 24, 8, 128)],
            [(24, 8, 128), (24, 8, 128), (8, 192, 128)],
            pos, state, kept, coarse_cf, *rows,
        )
        if turn < 3:
            state = over_tm(state, lambda x, y, c: (x + 1, y, c))

    new_starts, new_ends = call(
        last_kernel, [(3, 4, 128, 128), (3, 4, 128, 128)], [],
        pos, ends, arrived, kept, slab, *maps3,
    )
    return (new_starts[None], new_ends[None])


def solution(mesh):
    placed = (
        P("tm", None, "space", None, None),
        P(None, "space", None, None),
        P("space", None, None),
        P("space", None, None),
    )
    return jax.shard_map(
        shards,
        mesh=mesh,
        in_specs=placed,
        out_specs=(P("tm", None, "space", None, None), P("tm", None, "space", None, None)),
        check_vma=False,
    )
```

```python
import functools
from typing import NamedTuple

import jax
import jax.numpy as jnp
from jax import lax
from jax.experimental import pallas as pl
from jax.experimental.pallas import tpu as pltpu
from jax.sharding import PartitionSpec as P


SPECIES_K = (1.0, 0.6, 0.3)
DECAY = 0.5
FINE_DT = 0.1
COARSE_Q = 0.25
COARSE_DT = 0.4
HALF = 4
F32 = jnp.float32
EXACT = lax.Precision.HIGHEST


def coarse_maps(comps):
    def index(shape, axis):
        return lax.broadcasted_iota(jnp.int32, shape, axis)

    def ones(mask):
        return jnp.where(mask, 1.0, 0.0).astype(F32)

    wide, rows = (128, 128), comps * 32
    spread = ones(index(wide, 0) // 4 == index(wide, 1) // 4)
    row = index((comps * 8, rows), 1)
    fold = ones(row // 32 * 8 + row % 2 * 4 + row // 8 % 4 == index((comps * 8, rows), 0))
    keep = ones(index((rows, 128), 0) % 8 // 2 == index((rows, 128), 1) % 4)
    return spread, fold, keep


def fold_rows(rows, spread, fold, keep):
    wide = jnp.dot(rows, spread, precision=EXACT, preferred_element_type=F32) * keep
    return jnp.dot(fold, wide, precision=EXACT, preferred_element_type=F32) * (1.0 / 64.0)


def unfold_rows(coarse, spread, fold, keep):
    wide = lax.dot_general(
        fold, coarse, (((0,), (0,)), ((), ())), precision=EXACT, preferred_element_type=F32
    )
    return lax.dot_general(
        wide * keep, spread, (((1,), (1,)), ((), ())), precision=EXACT, preferred_element_type=F32
    )


def block_rows(load, comps):
    out = []
    for comp in range(comps):
        for yv in range(4):
            parts = [load(comp, z, 4 * yv + j) for z in range(4) for j in range(4)]
            while len(parts) > 1:
                parts = [a + b for a, b in zip(parts[::2], parts[1::2])]
            out.append(parts[0])
    return jnp.concatenate(out, 0)


def strided(ref, *lead):
    return lambda v: ref[(*lead, pl.ds(v, 8, stride=16), slice(None))]


def copy(src, dst, sem):
    moved = pltpu.make_async_copy(src, dst, sem)
    moved.start()
    return moved


def share_kernel(vel, dif, rate, down, up, sem):
    moved = []
    for out, quarter, first in ((down, place().quarters[0], 1), (up, place().quarters[1], 0)):
        rows = pl.ds(pl.multiple_of(quarter * 32, 32), 32)
        planes = pl.ds(first, 3)
        moved.append(copy(vel.at[:, planes, rows], out.at[pl.ds(0, 3)], sem.at[len(moved)]))
        moved.append(copy(dif.at[planes, rows], out.at[3], sem.at[len(moved)]))
        moved.append(copy(rate.at[planes, rows], out.at[4], sem.at[len(moved)]))
    for m in moved:
        m.wait()


def put_coefs(cf, plane, v, raw, scale):
    scaled = [w * scale for w in raw]
    for i, w in enumerate(scaled):
        cf[plane, i, v] = w
    cf[plane, 5, v] = 1.0 - (jnp.abs(scaled[0]) + jnp.abs(scaled[1]) + jnp.abs(scaled[2]))


def coefs_kernel(vel, dif, rate, *refs):
    pieces, (cf, thin, raw, sem) = refs[:8], refs[8:]
    core = place().core
    moved = []
    for side in range(2):
        for j in range(4):
            quarter = place().quarters[side]
            if j in (1, 3):
                quarter = lax.rem(quarter + 2, 4)
            if j >= 2:
                quarter = quarter + 1 - 2 * core
            rows = pl.ds(pl.multiple_of(quarter * 32, 32), 32)
            moved.append(copy(pieces[4 * side + j], raw.at[side, :, :, rows], sem.at[len(moved)]))

    def load(c, z, v):
        if c < 3:
            return strided(vel, c, z)(v)
        return strided(dif if c == 3 else rate, z)(v)

    @pl.loop(0, 4)
    def _(z):
        for v in range(16):
            put_coefs(cf, z + 3, v, [load(c, z, v) for c in range(5)], FINE_DT)

    thin[...] = fold_rows(
        block_rows(lambda c, z, v: cf[z + 3, c, v], 5), *coarse_maps(5)
    ) * (1.0 / FINE_DT)
    for m in moved:
        m.wait()

    has_low, has_high = edges()

    @pl.loop(0, 3)
    def _(z):
        for side, at, scale in ((0, 0, has_low), (1, 7, has_high)):
            for v in range(16):
                put_coefs(cf, z + at, v, [strided(raw, side, c, z)(v) for c in range(5)], FINE_DT * scale)


def pack_kernel(starts, pack):
    part = fold_rows(block_rows(lambda sp, z, v: strided(starts, sp, z)(v), 3), *coarse_maps(3))
    for sp in range(3):
        for z in range(4):
            for v in range(16):
                pack[sp * 64 + z * 16 + v] = strided(starts, sp, z)(v)
        pack[192 + sp] = part[8 * sp:8 * sp + 8]


def gate_kernel(*refs):
    del refs


def fine_cell(load, cf, p, v, dst):
    vel = [cf[p - 1, i, v] for i in range(3)]
    d = cf[p - 1, 3, v]
    base = cf[p - 1, 5, v]
    ahead = [w > 0.0 for w in vel]
    speed = [jnp.abs(w) for w in vel]
    new, old = [], []
    for sp in range(3):
        u = load(sp, p, v)
        old.append(u)
        pairs = (
            (pltpu.roll(u, 1, 1), pltpu.roll(u, 127, 1)),
            (
                load(sp, p, v - 1) if v > 0 else pltpu.roll(load(sp, p, 15), 1, 0),
                load(sp, p, v + 1) if v < 15 else pltpu.roll(load(sp, p, 0), 7, 0),
            ),
            (load(sp, p - 1, v), load(sp, p + 1, v)),
        )
        flow = [s * jnp.where(a, lo_, hi_) for s, a, (lo_, hi_) in zip(speed, ahead, pairs)]
        near = [lo_ + hi_ for lo_, hi_ in pairs]
        k = SPECIES_K[sp]
        mid = base - d * (6.0 * k)
        if sp == 2:
            mid = mid - FINE_DT * DECAY
        lap = (near[0] + near[1]) + near[2]
        new.append((mid * u + (d * k if k != 1.0 else d) * lap) + ((flow[0] + flow[1]) + flow[2]))
    r = cf[p - 1, 4, v] * old[0] * old[1]
    dst[0, p * 16 + v] = new[0] - r
    dst[1, p * 16 + v] = new[1] - r
    dst[2, p * 16 + v] = new[2] + r


def fine_step(src, dst, cf, lo, hi):
    @pl.loop(0, (hi - lo) // 2)
    def _(j):
        for v in range(16):
            for q in range(2):
                fine_cell(lambda sp, p, v: src[sp, p * 16 + v], cf, lo + 2 * j + q, v, dst)


def four_steps(low, own, high, has_low, has_high, buf_a, buf_b, cf):
    def load(sp, p, v):
        if p < 4:
            return low[sp * 64 + p * 16 + v] * has_low
        if p < 8:
            return own[sp * 64 + (p - 4) * 16 + v]
        return high[sp * 64 + (p - 8) * 16 + v] * has_high

    for p in range(1, 11):
        for v in range(16):
            fine_cell(load, cf, p, v, buf_a)
    fine_step(buf_a, buf_b, cf, 2, 10)
    fine_step(buf_b, buf_a, cf, 3, 9)
    fine_step(buf_a, buf_b, cf, 4, 8)


def plane_coefs(thin, y):
    vel = [thin[8 * c + y] * (COARSE_DT * COARSE_Q) for c in range(3)]
    d = thin[24 + y] * (COARSE_DT * COARSE_Q * COARSE_Q)
    up = [jnp.maximum(v, 0.0) for v in vel]
    down = [a - v for a, v in zip(up, vel)]
    out = []
    for sp, k in enumerate(SPECIES_K):
        kd = d * k
        total = 6.0 * kd
        for c in range(3):
            total = total + up[c] + down[c]
            out += [kd + up[c], kd + down[c]]
        out.append(1.0 - total - (COARSE_DT * DECAY if sp == 2 else 0.0))
    return out, thin[32 + y] * COARSE_DT


def coarse_plane_step(state, below, above, thin, has_low, has_high):
    lane = lax.broadcasted_iota(jnp.int32, (8, 128), 1) % 4
    sub = lax.broadcasted_iota(jnp.int32, (8, 128), 0)
    w, react = plane_coefs([thin[8 * c:8 * c + 8] for c in range(5) for _ in range(8)], 0)
    new = []
    for sp in range(3):
        u = state[sp]
        r = pltpu.roll(u, 1, 0)
        y_low = jnp.where(sub == 0, jnp.where(lane == 0, pltpu.roll(r, 125, 1), pltpu.roll(r, 1, 1)), r)
        r = pltpu.roll(u, 7, 0)
        y_high = jnp.where(sub == 7, jnp.where(lane == 3, pltpu.roll(r, 3, 1), pltpu.roll(r, 127, 1)), r)
        near = (pltpu.roll(u, 4, 1), pltpu.roll(u, 124, 1), y_low, y_high, below[sp] * has_low, above[sp] * has_high)
        val = w[7 * sp + 6] * u
        for i in range(6):
            val = val + w[7 * sp + i] * near[i]
        new.append(val)
    r = react * state[0] * state[1]
    return new[0] - r, new[1] - r, new[2] + r


class Place(NamedTuple):
    slice: jax.Array
    z: jax.Array
    group: jax.Array
    y: jax.Array
    core: jax.Array
    quarters: tuple


def place():
    tm = lax.axis_index("tm")
    x, y, core = tm // 8, tm // 2 % 4, tm % 2
    return Place(tm, lax.axis_index("space"), x, y, core, (y % 2 * 2 + core, x % 2 * 2 + core))


def edges():
    z = lax.axis_index("space")
    has_low = jnp.where(z > 0, 1.0, 0.0).astype(F32)
    has_high = jnp.where(z < lax.axis_size("space") - 1, 1.0, 0.0).astype(F32)
    return has_low, has_high


def coarse_rows(pack):
    return [pack[192 + sp] for sp in range(3)]


def first_kernel(thin, own, low, high, cf, out, buf_a, buf_b):
    has_low, has_high = edges()
    four_steps(low, own, high, has_low, has_high, buf_a, buf_b, cf)
    coarse = coarse_plane_step(coarse_rows(own), coarse_rows(low), coarse_rows(high), thin[...], has_low, has_high)
    for sp in range(3):
        out[pl.ds(64 * sp, 64)] = buf_b[sp, 64:128]
        out[192 + sp] = coarse[sp]


def second_kernel(thin, own, low, high, cf, pack, sent, buf_a, buf_b):
    has_low, has_high = edges()
    four_steps(low, own, high, has_low, has_high, buf_a, buf_b, cf)
    part = fold_rows(block_rows(lambda sp, z, v: buf_b[sp, 64 + 16 * z + v], 3), *coarse_maps(3))
    old = coarse_plane_step(coarse_rows(own), coarse_rows(low), coarse_rows(high), thin[...], has_low, has_high)
    first = place().slice == 0
    for sp in range(3):
        own_part = part[8 * sp:8 * sp + 8]
        pack[pl.ds(64 * sp, 64)] = buf_b[sp, 64:128]
        pack[192 + sp] = own_part
        diff = own_part - jnp.where(first, 0.0, old[sp])
        for z in range(8):
            sent[z, 8 * sp:8 * sp + 8] = diff
    for z in range(8):
        sent[z, 24:64] = thin[...]


def coarse_step(load, cf, store):
    lane = lax.broadcasted_iota(jnp.int32, (8, 128), 1) % 4
    rows = [[load(sp, y) for y in range(8)] for sp in range(3)]
    for y in range(8):
        new = []
        for sp in range(3):
            u = rows[sp][y]
            if y > 0:
                below = rows[sp][y - 1]
            else:
                below = jnp.where(lane == 0, pltpu.roll(rows[sp][7], 125, 1), pltpu.roll(rows[sp][7], 1, 1))
            if y < 7:
                above = rows[sp][y + 1]
            else:
                above = jnp.where(lane == 3, pltpu.roll(rows[sp][0], 3, 1), pltpu.roll(rows[sp][0], 127, 1))
            w = [cf[7 * sp + i, y] for i in range(7)]
            val = (w[6] * u + w[2] * below) + (w[3] * above + w[0] * pltpu.roll(u, 4, 1)) + (
                w[1] * pltpu.roll(u, 124, 1) + (w[4] * pltpu.roll(u, 1, 0) + w[5] * pltpu.roll(u, 7, 0)))
            new.append(val)
        r = cf[21, y] * rows[0][y] * rows[1][y]
        store(0, y, new[0] - r)
        store(1, y, new[1] - r)
        store(2, y, new[2] + r)


def own_row(z_at, ref):
    here = lax.broadcasted_iota(jnp.int32, (24, 8, 128), 1) == z_at
    return jnp.sum(jnp.where(here, ref[...], 0.0), axis=1)


def weights_kernel(thin, cf):
    sub = lax.broadcasted_iota(jnp.int32, (8, 128), 0)
    rows = [jnp.concatenate([thin[z, r:r + 1] for z in range(8)], 0) for r in range(40)]
    for y in range(8):
        w, react = plane_coefs(rows, y)
        for i, val in enumerate(w):
            if i % 7 == 4:
                val = jnp.where(sub == 0, 0.0, val)
            if i % 7 == 5:
                val = jnp.where(sub == 7, 0.0, val)
            cf[i, y] = val
        cf[21, y] = react


def run_chain(defects, c_in, cf, keep, state, tmp, line):
    here = place()
    at_y, core = here.y, here.core
    for k in range(4):
        slot = lax.rem(at_y - k + 4, 4) * 2
        line[slot + core] = defects[k][...]
        line[slot + 1 - core] = defects[4 + k][...]
    state[...] = jnp.zeros_like(state) if c_in is None else c_in[...]
    own = 2 * at_y + core

    def put(sp, y, val):
        tmp[8 * sp + y] = val

    @pl.loop(0, 8)
    def _(i):
        @pl.when(i == own)
        def _():
            keep[0] = own_row(here.z, state)

        def add(sp, y, val):
            r = 8 * sp + y
            state[r] = val + line[i, pl.ds(r, 8, stride=24), :]

        coarse_step(lambda sp, y: state[8 * sp + y], cf, put)
        coarse_step(lambda sp, y: tmp[8 * sp + y], cf, add)

        @pl.when(i == own)
        def _():
            keep[1] = own_row(here.z, state)


def chain_kernel(turn, cf, *refs):
    refs = list(refs)
    c_in, kept = (refs.pop(0), refs.pop(0)) if turn else (None, None)
    defects, (c_out, keep, state, tmp, line) = refs[:8], refs[8:]

    @pl.when(place().group != turn)
    def _():
        if turn:
            c_out[...] = c_in[...]
            keep[...] = kept[...]
        else:
            c_out[...] = jnp.zeros_like(c_out)
            keep[...] = jnp.zeros_like(keep)

    @pl.when(place().group == turn)
    def _():
        run_chain(defects, c_in, cf, keep, state, tmp, line)
        c_out[...] = state[...]


def last_kernel(turn, cf, c_in, kept, *refs):
    defects, refs = refs[:8], refs[8:]
    (ends, arrived, starts, new_starts, new_ends,
     keep, state, tmp, line, packs, outs, in_sem, out_sem) = refs
    packed = [copy(arrived, packs.at[0], in_sem.at[0]), copy(ends, packs.at[1], in_sem.at[1])]

    @pl.when(place().group != turn)
    def _():
        keep[...] = kept[...]

    @pl.when(place().group == turn)
    def _():
        run_chain(defects, c_in, cf, keep, state, tmp, line)

    for m in packed:
        m.wait()
    first = place().slice == 0

    @pl.when(first)
    def _():
        copy(starts, outs.at[0], out_sem.at[0]).wait()

    for which in range(2):
        def fill(which=which):
            own = keep[which] - jnp.concatenate([packs[which, 192 + sp] for sp in range(3)], 0)
            back = unfold_rows(own, *coarse_maps(3))
            for sp in range(3):
                for yv in range(4):
                    at = (sp * 4 + yv) * 8
                    cell = back[at:at + 8]
                    for z in range(4):
                        for j in range(4):
                            v = 4 * yv + j
                            outs[which, sp, z, pl.ds(v, 8, stride=16), :] = packs[which, sp * 64 + z * 16 + v] + cell

        if which == 0:
            pl.when(jnp.logical_not(first))(fill)
        else:
            fill()
        copy(outs.at[which], (new_starts, new_ends)[which], out_sem.at[which])
    for which in range(2):
        pltpu.make_async_copy(outs.at[which], (new_starts, new_ends)[which], out_sem.at[which]).wait()


NEAR, FREE = pltpu.VMEM, pl.ANY


def call(kernel, outs, scratch, *args, limit=24, alias=None, cost=2):
    args = [a if isinstance(a, tuple) else (a, NEAR) for a in args]
    return pl.pallas_call(
        kernel,
        out_shape=[jax.ShapeDtypeStruct(s, F32) for s, _ in outs],
        in_specs=[pl.BlockSpec(memory_space=space) for _, space in args],
        out_specs=[pl.BlockSpec(memory_space=space) for _, space in outs],
        scratch_shapes=[
            pltpu.SemaphoreType.DMA((s,)) if isinstance(s, int) else pltpu.VMEM(s, F32) for s in scratch
        ],
        input_output_aliases=alias or {},
        cost_estimate=pl.CostEstimate(flops=0, bytes_accessed=cost * 3_600_000, transcendentals=0),
        compiler_params=pltpu.CompilerParams(vmem_limit_bytes=limit * 1024 * 1024),
    )(*[a for a, _ in args])


def over_z(block, move):
    count = lax.axis_size("space")
    return lax.ppermute(block, "space", [(i, move(i) % count) for i in range(count)])


def both_ways(block):
    return over_z(block, lambda i: i + 1), over_z(block, lambda i: i - 1)


def over_tm(block, move):
    pairs = []
    for i in range(32):
        x, y, c = i // 8, i // 2 % 4, i % 2
        x, y, c = move(x, y, c)
        pairs.append((i, (x % 4) * 8 + (y % 4) * 2 + c))
    return lax.ppermute(block, "tm", pairs)


def shards(starts, velocity, diffusivity, rate):
    slab = starts[0]
    free = lambda *arrays: [(a, FREE) for a in arrays]

    cf_shape, pack_shape, piece_shape = (10, 6, 16, 8, 128), (195, 8, 128), (5, 3, 32, 128)
    down, up = call(
        share_kernel, [(piece_shape, NEAR)] * 2, [6], *free(velocity, diffusivity, rate), limit=60
    )
    c_low = over_z(down, lambda i: i + 1)
    c_high = over_z(up, lambda i: i - 1)
    (own,) = call(pack_kernel, [(pack_shape, NEAR)], [], slab)
    (own,) = call(gate_kernel, [(pack_shape, FREE)], [], *free(own, c_low, c_high), alias={0: 0})
    low, high = both_ways(own)
    swap = lambda block: over_tm(block, lambda x, y, c: (x, y, 1 - c))
    side_low = [c_low, over_tm(c_low, lambda x, y, c: (x, y ^ 1, c))]
    side_high = [c_high, over_tm(c_high, lambda x, y, c: (x ^ 1, y, c))]
    pieces = side_low + [swap(p) for p in side_low] + side_high + [swap(p) for p in side_high]
    cf, thin = call(
        coefs_kernel, [(cf_shape, NEAR), ((40, 128), NEAR)], [(2, 5, 3, 128, 128), 8],
        velocity, diffusivity, rate, *free(*pieces),
    )

    fine_scratch = [(3, 192, 8, 128), (3, 192, 8, 128)]
    (middle,) = call(first_kernel, [(pack_shape, NEAR)], fine_scratch, thin, own, low, high, cf, cost=6)
    low, high = both_ways(middle)
    pack, sent = call(
        second_kernel, [(pack_shape, NEAR), ((8, 64, 128), NEAR)], fine_scratch,
        thin, middle, low, high, cf, cost=6,
    )

    arrived = over_tm(pack, lambda x, y, c: (x + (y + c) // 4, y + c, 1 - c))
    got = lax.all_to_all(sent, "space", 0, 0, tiled=True)
    defect = got[:, :24].reshape(192, 128)
    (coarse_cf,) = call(weights_kernel, [((22, 8, 8, 128), NEAR)], [], got[:, 24:])
    rows = [defect] + [over_tm(defect, lambda x, y, c, k=k: (x, y + k, c)) for k in (1, 2, 3)]
    rows += [swap(r) for r in rows]

    grid = (24, 8, 128)
    chain_scratch = [grid, grid, (8, 192, 128)]
    state = ()
    for turn in range(3):
        out, kept = call(
            functools.partial(chain_kernel, turn), [(grid, NEAR), ((2, 24, 128), NEAR)], chain_scratch,
            coarse_cf, *state, *rows,
        )
        state = (over_tm(out, lambda x, y, c: (x + 1, y, c)), kept)
    new_starts, new_ends = call(
        functools.partial(last_kernel, 3), [((3, 4, 128, 128), FREE)] * 2,
        [(2, 24, 128)] + chain_scratch + [(2, 195, 8, 128), (2, 3, 4, 128, 128), 2, 2],
        coarse_cf, *state, *rows, *free(pack, arrived, slab),
    )
    return (new_starts[None], new_ends[None])


def solution(mesh):
    placed = (
        P("tm", None, "space", None, None),
        P(None, "space", None, None),
        P("space", None, None),
        P("space", None, None),
    )
    return jax.shard_map(
        shards,
        mesh=mesh,
        in_specs=placed,
        out_specs=(P("tm", None, "space", None, None), P("tm", None, "space", None, None)),
        check_vma=False,
    )
```

```python
import functools
from typing import NamedTuple

import jax
import jax.numpy as jnp
from jax import lax
from jax.experimental import pallas as pl
from jax.experimental.pallas import tpu as pltpu
from jax.sharding import PartitionSpec as P


SPECIES_K = (1.0, 0.6, 0.3)
DECAY = 0.5
FINE_DT = 0.1
COARSE_Q = 0.25
COARSE_DT = 0.4
HALF = 4
F32 = jnp.float32
EXACT = lax.Precision.HIGHEST


def coarse_maps(comps):
    def index(shape, axis):
        return lax.broadcasted_iota(jnp.int32, shape, axis)

    def ones(mask):
        return jnp.where(mask, 1.0, 0.0).astype(F32)

    wide, rows = (128, 128), comps * 32
    spread = ones(index(wide, 0) // 4 == index(wide, 1) // 4)
    row = index((comps * 8, rows), 1)
    fold = ones(row // 32 * 8 + row % 2 * 4 + row // 8 % 4 == index((comps * 8, rows), 0))
    keep = ones(index((rows, 128), 0) % 8 // 2 == index((rows, 128), 1) % 4)
    return spread, fold, keep


def fold_rows(rows, spread, fold, keep):
    wide = jnp.dot(rows, spread, precision=EXACT, preferred_element_type=F32) * keep
    return jnp.dot(fold, wide, precision=EXACT, preferred_element_type=F32) * (1.0 / 64.0)


def unfold_rows(coarse, spread, fold, keep):
    wide = lax.dot_general(
        fold, coarse, (((0,), (0,)), ((), ())), precision=EXACT, preferred_element_type=F32
    )
    return lax.dot_general(
        wide * keep, spread, (((1,), (1,)), ((), ())), precision=EXACT, preferred_element_type=F32
    )


def block_rows(load, comps):
    out = []
    for comp in range(comps):
        for yv in range(4):
            parts = [load(comp, z, 4 * yv + j) for z in range(4) for j in range(4)]
            while len(parts) > 1:
                parts = [a + b for a, b in zip(parts[::2], parts[1::2])]
            out.append(parts[0])
    return jnp.concatenate(out, 0)


def strided(ref, *lead):
    return lambda v: ref[(*lead, pl.ds(v, 8, stride=16), slice(None))]


def copy(src, dst, sem):
    moved = pltpu.make_async_copy(src, dst, sem)
    moved.start()
    return moved


def odd_slab():
    return lax.rem(lax.axis_index("space"), 2)


def share_kernel(vel, dif, rate, first, second, sem):
    moved = []
    for out, quarter, to_next in ((first, place().quarters[0], odd_slab() == 0), (second, place().quarters[1], odd_slab() == 1)):
        rows = pl.ds(pl.multiple_of(quarter * 32, 32), 32)
        planes = pl.ds(jnp.where(to_next, 1, 0), 3)
        moved.append(copy(vel.at[:, planes, rows], out.at[pl.ds(0, 3)], sem.at[len(moved)]))
        moved.append(copy(dif.at[planes, rows], out.at[3], sem.at[len(moved)]))
        moved.append(copy(rate.at[planes, rows], out.at[4], sem.at[len(moved)]))
    for m in moved:
        m.wait()


def put_coefs(cf, plane, v, raw, scale):
    vel = [w * scale for w in raw[:3]]
    base = 1.0 - (jnp.abs(vel[0]) + jnp.abs(vel[1]) + jnp.abs(vel[2]))
    d = raw[3] * scale
    cf[plane, 3, v] = d
    cf[plane, 4, v] = raw[4] * scale
    for i in range(3):
        cf[plane, i, v] = vel[i]
        cf[plane, 5 + i, v] = base - d * (6.0 * SPECIES_K[i]) - (FINE_DT * DECAY if i == 2 else 0.0)


def coefs_kernel(vel, dif, rate, *refs):
    pieces, (cf, thin, part, raw, sem) = refs[:8], refs[8:]
    core = place().core
    moved = []
    for pair in range(2):
        side = 1 - odd_slab() if pair == 0 else odd_slab()
        for j in range(4):
            quarter = place().quarters[pair]
            if j in (1, 3):
                quarter = lax.rem(quarter + 2, 4)
            if j >= 2:
                quarter = quarter + 1 - 2 * core
            rows = pl.ds(pl.multiple_of(quarter * 32, 32), 32)
            moved.append(copy(pieces[4 * pair + j], raw.at[side, :, :, rows], sem.at[len(moved)]))

    def load(c, z, v):
        if c < 3:
            return strided(vel, c, z)(v)
        return strided(dif if c == 3 else rate, z)(v)

    @pl.loop(0, 4)
    def _(z):
        for v in range(16):
            put_coefs(cf, z + 3, v, [load(c, z, v) for c in range(5)], FINE_DT)

    thin[...] = fold_rows(
        block_rows(lambda c, z, v: cf[z + 3, c, v], 5), *coarse_maps(5)
    ) * (1.0 / FINE_DT)
    own = place().y * 2 + core
    rows = jnp.zeros((5, 128), F32)
    for k in range(8):
        rows = jnp.where(own == k, thin[5 * k:5 * k + 5], rows)
    part[...] = jnp.concatenate([rows, jnp.zeros((3, 128), F32)], 0)
    for m in moved:
        m.wait()

    has_low, has_high = edges()

    @pl.loop(0, 3)
    def _(z):
        for side, at, scale in ((0, 0, has_low), (1, 7, has_high)):
            for v in range(16):
                put_coefs(cf, z + at, v, [strided(raw, side, c, z)(v) for c in range(5)], FINE_DT * scale)


def pack_kernel(starts, pack):
    part = fold_rows(block_rows(lambda sp, z, v: strided(starts, sp, z)(v), 3), *coarse_maps(3))
    for sp in range(3):
        for z in range(4):
            for v in range(16):
                pack[sp * 64 + z * 16 + v] = strided(starts, sp, z)(v)
        pack[192 + sp] = part[8 * sp:8 * sp + 8]


def gate_kernel(*refs):
    del refs


def fine_cell(load, cf, p, v, dst):
    vel = [cf[p - 1, i, v] for i in range(3)]
    d = cf[p - 1, 3, v]
    ahead = [w > 0.0 for w in vel]
    speed = [jnp.abs(w) for w in vel]
    new, old = [], []
    for sp in range(3):
        u = load(sp, p, v)
        old.append(u)
        pairs = (
            (pltpu.roll(u, 1, 1), pltpu.roll(u, 127, 1)),
            (
                load(sp, p, v - 1) if v > 0 else pltpu.roll(load(sp, p, 15), 1, 0),
                load(sp, p, v + 1) if v < 15 else pltpu.roll(load(sp, p, 0), 7, 0),
            ),
            (load(sp, p - 1, v), load(sp, p + 1, v)),
        )
        flow = [s * jnp.where(a, lo_, hi_) for s, a, (lo_, hi_) in zip(speed, ahead, pairs)]
        near = [lo_ + hi_ for lo_, hi_ in pairs]
        lap = (near[0] + near[1]) + near[2]
        new.append((cf[p - 1, 5 + sp, v] * u + (d if sp == 0 else d * SPECIES_K[sp]) * lap) + ((flow[0] + flow[1]) + flow[2]))
    r = cf[p - 1, 4, v] * old[0] * old[1]
    dst[0, p * 16 + v] = new[0] - r
    dst[1, p * 16 + v] = new[1] - r
    dst[2, p * 16 + v] = new[2] + r


def fine_step(load, cf, lo, hi, dst):
    for v in range(16):
        for p in range(lo, hi):
            fine_cell(load, cf, p, v, dst)


def four_steps(load, buf_a, buf_b, cf):
    has_low, has_high = edges()

    def masked(sp, p, v):
        val = load(sp, p, v)
        return val * has_low if p < 4 else val * has_high if p >= 8 else val

    def held(buf):
        return lambda sp, p, v: buf[sp, p * 16 + v]

    fine_step(masked, cf, 1, 11, buf_a)
    fine_step(held(buf_a), cf, 2, 10, buf_b)
    fine_step(held(buf_b), cf, 3, 9, buf_a)
    fine_step(held(buf_a), cf, 4, 8, buf_b)


def plane_coefs(thin, y):
    vel = [thin[8 * c + y] * (COARSE_DT * COARSE_Q) for c in range(3)]
    d = thin[24 + y] * (COARSE_DT * COARSE_Q * COARSE_Q)
    up = [jnp.maximum(v, 0.0) for v in vel]
    down = [a - v for a, v in zip(up, vel)]
    out = []
    for sp, k in enumerate(SPECIES_K):
        kd = d * k
        total = 6.0 * kd
        for c in range(3):
            total = total + up[c] + down[c]
            out += [kd + up[c], kd + down[c]]
        out.append(1.0 - total - (COARSE_DT * DECAY if sp == 2 else 0.0))
    return out, thin[32 + y] * COARSE_DT


def coarse_plane_step(state, below, above, thin):
    has_low, has_high = edges()
    lane = lax.broadcasted_iota(jnp.int32, (8, 128), 1) % 4
    sub = lax.broadcasted_iota(jnp.int32, (8, 128), 0)
    w, react = plane_coefs([thin[8 * c:8 * c + 8] for c in range(5) for _ in range(8)], 0)
    new = []
    for sp in range(3):
        u = state[sp]
        r = pltpu.roll(u, 1, 0)
        y_low = jnp.where(sub == 0, jnp.where(lane == 0, pltpu.roll(r, 125, 1), pltpu.roll(r, 1, 1)), r)
        r = pltpu.roll(u, 7, 0)
        y_high = jnp.where(sub == 7, jnp.where(lane == 3, pltpu.roll(r, 3, 1), pltpu.roll(r, 127, 1)), r)
        near = (pltpu.roll(u, 4, 1), pltpu.roll(u, 124, 1), y_low, y_high, below[sp] * has_low, above[sp] * has_high)
        val = w[7 * sp + 6] * u
        for i in range(6):
            val = val + w[7 * sp + i] * near[i]
        new.append(val)
    r = react * state[0] * state[1]
    return new[0] - r, new[1] - r, new[2] + r


class Place(NamedTuple):
    slice: jax.Array
    z: jax.Array
    group: jax.Array
    y: jax.Array
    core: jax.Array
    quarters: tuple


def place():
    tm = lax.axis_index("tm")
    x, y, core = tm // 8, tm // 2 % 4, tm % 2
    return Place(tm, lax.axis_index("space"), x, y, core, (y % 2 * 2 + core, x % 2 * 2 + core))


def edges():
    z = lax.axis_index("space")
    has_low = jnp.where(z > 0, 1.0, 0.0).astype(F32)
    has_high = jnp.where(z < lax.axis_size("space") - 1, 1.0, 0.0).astype(F32)
    return has_low, has_high


def coarse_rows(pack, at):
    return [pack[at + sp] for sp in range(3)]


def slabs(low, own, high):
    return lambda sp, p, v: (low, own, high)[p // 4][sp * 64 + p % 4 * 16 + v]


def first_kernel(thin, own, low, high, cf, out, buf_a, buf_b):
    four_steps(slabs(low, own, high), buf_a, buf_b, cf)
    coarse = coarse_plane_step(*[coarse_rows(r, 192) for r in (own, low, high)], thin[...])
    for sp in range(3):
        out[pl.ds(64 * sp, 64)] = buf_b[sp, 64:128]
        out[192 + sp] = coarse[sp]


def second_kernel(thin, part_cf, own, low, high, cf, pack, sent, buf_a, buf_b):
    four_steps(slabs(low, own, high), buf_a, buf_b, cf)
    part = fold_rows(block_rows(lambda sp, z, v: buf_b[sp, 64 + 16 * z + v], 3), *coarse_maps(3))
    old = coarse_plane_step(*[coarse_rows(r, 192) for r in (own, low, high)], thin[...])
    first = place().slice == 0
    block = []
    for sp in range(3):
        own_part = part[8 * sp:8 * sp + 8]
        pack[pl.ds(64 * sp, 64)] = buf_b[sp, 64:128]
        pack[192 + sp] = own_part
        block.append(own_part - jnp.where(first, 0.0, old[sp]))
    block.append(part_cf[...])
    for to in range(8):
        for j in range(4):
            sent[to, 8 * j:8 * j + 8] = block[j]


def coarse_step(rows, cf):
    lane = lax.broadcasted_iota(jnp.int32, (8, 128), 1) % 4
    out = [[], [], []]
    for y in range(8):
        new = []
        for sp in range(3):
            u = rows[sp][y]
            if y > 0:
                below = rows[sp][y - 1]
            else:
                below = jnp.where(lane == 0, pltpu.roll(rows[sp][7], 125, 1), pltpu.roll(rows[sp][7], 1, 1))
            if y < 7:
                above = rows[sp][y + 1]
            else:
                above = jnp.where(lane == 3, pltpu.roll(rows[sp][0], 3, 1), pltpu.roll(rows[sp][0], 127, 1))
            w = [cf[7 * sp + i, y] for i in range(7)]
            val = (w[6] * u + w[2] * below) + (w[3] * above + w[0] * pltpu.roll(u, 4, 1)) + (
                w[1] * pltpu.roll(u, 124, 1) + (w[4] * pltpu.roll(u, 1, 0) + w[5] * pltpu.roll(u, 7, 0)))
            new.append(val)
        r = cf[21, y] * rows[0][y] * rows[1][y]
        for sp, val in enumerate((new[0] - r, new[1] - r, new[2] + r)):
            out[sp].append(val)
    return out


def own_row(z_at, state):
    here = lax.broadcasted_iota(jnp.int32, (24, 8, 128), 1) == z_at
    return jnp.sum(jnp.where(here, state, 0.0), axis=1)


def weights_kernel(*refs):
    got, (after, cf, line) = refs[:8], refs[8:]
    del after
    here = place()
    for k in range(4):
        slot = lax.rem(here.y - k + 4, 4) * 2
        line[slot + here.core] = got[k][...]
        line[slot + 1 - here.core] = got[4 + k][...]
    sub = lax.broadcasted_iota(jnp.int32, (8, 128), 0)
    rows = [line[r // 5, pl.ds(24 + r % 5, 8, stride=32), :] for r in range(40)]
    for y in range(8):
        w, react = plane_coefs(rows, y)
        for i, val in enumerate(w):
            if i % 7 == 4:
                val = jnp.where(sub == 0, 0.0, val)
            if i % 7 == 5:
                val = jnp.where(sub == 7, 0.0, val)
            cf[i, y] = val
        cf[21, y] = react


def run_chain(line, c_in, cf, keep, states):
    here = place()

    def put(i, rows):
        for sp in range(3):
            for y in range(8):
                states[i, 8 * sp + y] = rows[sp][y]

    zero = jnp.zeros((8, 128), F32)
    rows = [[zero if c_in is None else c_in[8 * sp + y] for y in range(8)] for sp in range(3)]
    put(0, rows)
    for i in range(8):
        rows = coarse_step(coarse_step(rows, cf), cf)
        rows = [
            [rows[sp][y] + line[i, pl.ds(8 * sp + y, 8, stride=32), :] for y in range(8)] for sp in range(3)
        ]
        put(i + 1, rows)
    own = 2 * here.y + here.core
    for j in range(2):
        keep[j] = states[own + j]


def chain_kernel(turn, cf, *refs):
    refs = list(refs)
    c_in, kept = (refs.pop(0), refs.pop(0)) if turn else (None, None)
    line, c_out, keep, states = refs

    @pl.when(place().group != turn)
    def _():
        if turn:
            c_out[...] = c_in[...]
            keep[...] = kept[...]
        else:
            c_out[...] = jnp.zeros_like(c_out)
            keep[...] = jnp.zeros_like(keep)

    @pl.when(place().group == turn)
    def _():
        run_chain(line, c_in, cf, keep, states)
        c_out[...] = states[8]


def last_kernel(
    turn, cf, c_in, kept, line, ends, arrived, starts, new_starts, new_ends,
    keep, states, packs, outs, in_sem, out_sem,
):
    packed = [copy(arrived, packs.at[0], in_sem.at[0]), copy(ends, packs.at[1], in_sem.at[1])]

    @pl.when(place().group != turn)
    def _():
        keep[...] = kept[...]

    @pl.when(place().group == turn)
    def _():
        run_chain(line, c_in, cf, keep, states)

    for m in packed:
        m.wait()
    first = place().slice == 0

    @pl.when(first)
    def _():
        copy(starts, outs.at[0], out_sem.at[0]).wait()

    z_at = lax.axis_index("space")
    own = [
        own_row(z_at, keep[which]) - jnp.concatenate([packs[which, 192 + sp] for sp in range(3)], 0)
        for which in range(2)
    ]
    back = unfold_rows(jnp.concatenate(own, 0), *coarse_maps(6))
    for which, dst in ((1, new_ends), (0, new_starts)):
        for sp in range(3):
            def fill(which=which, sp=sp):
                for yv in range(4):
                    at = ((which * 3 + sp) * 4 + yv) * 8
                    cell = back[at:at + 8]
                    for z in range(4):
                        for j in range(4):
                            v = 4 * yv + j
                            outs[which, sp, z, pl.ds(v, 8, stride=16), :] = packs[which, sp * 64 + z * 16 + v] + cell

            if which == 0:
                pl.when(jnp.logical_not(first))(fill)
            else:
                fill()
            copy(outs.at[which, sp], dst.at[sp], out_sem.at[3 * which + sp])
    for which, dst in ((1, new_ends), (0, new_starts)):
        for sp in range(3):
            pltpu.make_async_copy(outs.at[which, sp], dst.at[sp], out_sem.at[3 * which + sp]).wait()


NEAR, FREE = pltpu.VMEM, pl.ANY


def call(kernel, outs, scratch, *args, limit=24, alias=None, cost=2):
    args = [a if isinstance(a, tuple) else (a, NEAR) for a in args]
    return pl.pallas_call(
        kernel,
        out_shape=[jax.ShapeDtypeStruct(s, F32) for s, _ in outs],
        in_specs=[pl.BlockSpec(memory_space=space) for _, space in args],
        out_specs=[pl.BlockSpec(memory_space=space) for _, space in outs],
        scratch_shapes=[
            pltpu.SemaphoreType.DMA((s,)) if isinstance(s, int) else pltpu.VMEM(s, F32) for s in scratch
        ],
        input_output_aliases=alias or {},
        cost_estimate=pl.CostEstimate(flops=int(cost * 1e9), bytes_accessed=1_000_000, transcendentals=0),
        compiler_params=pltpu.CompilerParams(vmem_limit_bytes=limit * 1024 * 1024),
    )(*[a for a, _ in args])


def over_z(block, move):
    count = lax.axis_size("space")
    return lax.ppermute(block, "space", [(i, move(i) % count) for i in range(count)])


def over_tm(block, move):
    pairs = []
    for i in range(32):
        x, y, c = move(i // 8, i // 2 % 4, i % 2)
        pairs.append((i, (x % 4) * 8 + (y % 4) * 2 + c))
    return lax.ppermute(block, "tm", pairs)


def shards(starts, velocity, diffusivity, rate):
    slab = starts[0]
    free = lambda *arrays: [(a, FREE) for a in arrays]

    cf_shape, pack_shape, piece_shape = (10, 8, 16, 8, 128), (195, 8, 128), (5, 3, 32, 128)
    up_by, down_by = (lambda i: i + 1), (lambda i: i - 1)
    first, second = call(
        share_kernel, [(piece_shape, NEAR)] * 2, [6], *free(velocity, diffusivity, rate), limit=60
    )
    first = over_z(first, lambda i: i ^ 1)
    second = over_z(second, lambda i: ((i + 1) ^ 1) - 1)
    (own,) = call(pack_kernel, [(pack_shape, NEAR)], [], slab)
    low, high = over_z(own, up_by), over_z(own, down_by)
    swap = lambda block: over_tm(block, lambda x, y, c: (x, y, 1 - c))
    first = [first, over_tm(first, lambda x, y, c: (x, y ^ 1, c))]
    second = [second, over_tm(second, lambda x, y, c: (x ^ 1, y, c))]
    pieces = first + [swap(p) for p in first] + second + [swap(p) for p in second]
    cf, thin, part_cf = call(
        coefs_kernel, [(cf_shape, NEAR), ((40, 128), NEAR), ((8, 128), NEAR)], [(2, 5, 3, 128, 128), 8],
        velocity, diffusivity, rate, *free(*pieces),
    )

    fine_scratch = [(3, 192, 8, 128), (3, 192, 8, 128)]
    (middle,) = call(first_kernel, [(pack_shape, NEAR)], fine_scratch, thin, own, low, high, cf, cost=6)
    low, high = over_z(middle, up_by), over_z(middle, down_by)
    pack, sent = call(
        second_kernel, [(pack_shape, NEAR), ((8, 32, 128), NEAR)], fine_scratch,
        thin, part_cf, middle, low, high, cf, cost=6,
    )

    arrived = over_tm(pack, lambda x, y, c: (x + (y + c) // 4, y + c, 1 - c))
    defect = lax.all_to_all(sent, "space", 0, 0, tiled=True).reshape(256, 128)
    two = over_tm(defect, lambda x, y, c: (x, y + 2, c))
    one, three = [over_tm(defect, lambda x, y, c, k=k: (x, y + k, c)) for k in (1, 3)]
    rows = [defect, one, two, three]
    coarse_cf, line = call(
        weights_kernel, [((22, 8, 8, 128), NEAR), ((8, 256, 128), NEAR)], [],
        *rows, *[swap(r) for r in rows], *free(arrived),
    )

    grid = (24, 8, 128)
    chain_scratch = [(9, 24, 8, 128)]
    state = ()
    for turn in range(3):
        out, kept = call(
            functools.partial(chain_kernel, turn), [(grid, NEAR), ((2, 24, 8, 128), NEAR)], chain_scratch,
            coarse_cf, *state, line,
        )
        state = (over_tm(out, lambda x, y, c: (x + 1, y, c)), kept)
    new_starts, new_ends = call(
        functools.partial(last_kernel, 3), [((3, 4, 128, 128), FREE)] * 2,
        [(2, 24, 8, 128)] + chain_scratch + [(2, 195, 8, 128), (2, 3, 4, 128, 128), 2, 6],
        coarse_cf, *state, line, *free(pack, arrived, slab),
    )
    return (new_starts[None], new_ends[None])


def solution(mesh):
    placed = (
        P("tm", None, "space", None, None),
        P(None, "space", None, None),
        P("space", None, None),
        P("space", None, None),
    )
    return jax.shard_map(
        shards,
        mesh=mesh,
        in_specs=placed,
        out_specs=(P("tm", None, "space", None, None), P("tm", None, "space", None, None)),
        check_vma=False,
    )
```
